32 devices in a mesh: section: 2 (over x), dp: 4 (over z), tensor: 4 (over y, core).
Axes of the slice: x: 2, y: 2, z: 4, core: 2. Of those that a mesh axis runs over, the one named last changes fastest.
Arguments:
- source: bfloat16 [8, 2048, 768], P('dp'), may hold values from -6 to 6
- target: bfloat16 [8, 1024, 768], P('dp'), may hold values from -6 to 6
- src_len: int32 [8], P('dp'), may hold values from 1025 to 2048, as said below
- tgt_len: int32 [8], P('dp'), may hold values from 513 to 1024, as said below
- global_mask: int32 [8, 2048], P('dp'), may hold values 0 or 1
- attn_w: bfloat16 [2, 768, 3, 768], P('section', 'dp', None, 'tensor'), may hold values from -0.21875 to 0.21875
- proj_w: bfloat16 [2, 768, 768], P('section', 'tensor', 'dp'), may hold values from -3.5 to 3.5
- cross_w: bfloat16 [2, 768, 2, 768], P('section', 'dp', None, 'tensor'), may hold values from -4 to 4
- up_w: bfloat16 [2, 768, 3072], P('section', 'dp', 'tensor'), may hold values from -0.21875 to 0.21875
- down_w: bfloat16 [2, 3072, 768], P('section', 'tensor', 'dp'), may hold values from -0.109375 to 0.109375
- norms: float32 [2, 3, 2, 768], P('section'), may hold values from -1 to 1.4
- dec_cot: bfloat16 [8, 1024, 768], P('dp'), may hold values from -6 to 6
Outputs:
- dec_out: bfloat16 [8, 1024, 768], P('dp')
- source_grad: bfloat16 [8, 2048, 768], P('dp')
- target_grad: bfloat16 [8, 1024, 768], P('dp')
- grad_attn: float32 [2, 768, 3, 768], P('section', 'dp', None, 'tensor')
- grad_proj: float32 [2, 768, 768], P('section', 'tensor', 'dp')
- grad_cross: float32 [2, 768, 2, 768], P('section', 'dp', None, 'tensor')
- grad_up: float32 [2, 768, 3072], P('section', 'dp', 'tensor')
- grad_down: float32 [2, 3072, 768], P('section', 'tensor', 'dp')
- grad_norms: float32 [2, 3, 2, 768], P('section', None, None, 'dp')
The draws below stay inside these ranges and needn't reach their ends.
Inputs may be any that keep to these rules, and one draw needn't show every extreme that they name: `src_len`: every sequence uses more than half of its 2048 padded tokens; some sequence uses all 2048. `tgt_len`: every target uses more than half of its 1024 tokens; some target uses all 1024.
All inputs are finite; a program needn't handle non-finite values. No bound on the sum of `global_mask` on one device may be relied on, other than what follows from the above.
Results may differ from the reference program's by a relative error of at most 0.023.
Values may be sent and summed in bfloat16 or wider, within the bound.
No kernel may reach another device: no remote copies, remote signals or barrier semaphores. Data moves between devices by JAX's collectives and lax.ppermute only.
A program may use at most 512 MiB of HBM per device.

```python
import jax
import jax.numpy as jnp
from jax import lax

D = 768
HD = 64
FF = 3072
WINDOW = 1024
TGT = 1024
SRC = 2048
SEQS = 8


def ragged_lengths(key, longest):
    first, second = jax.random.split(key)
    lengths = jax.random.randint(first, (SEQS,), longest // 2 + 1, longest + 1)
    spot = jax.random.randint(second, (), 0, SEQS)
    seats = jnp.arange(SEQS)
    lengths = jnp.where(seats == spot, longest, lengths)
    lengths = jnp.where(seats == (spot + 1) % SEQS, longest // 2 + 1, lengths)
    return lengths.astype(jnp.int32)


def draw_src_len(key, part):
    key = jax.random.fold_in(key, 11)
    return ragged_lengths(key, SRC)


def draw_tgt_len(key, part):
    key = jax.random.fold_in(key, 12)
    return ragged_lengths(key, TGT)


def draw_cross_w(key, part):
    key = jax.random.fold_in(key, 13)
    base = jnp.clip(jax.random.normal(key, (2, D, 2, D), jnp.float32), -4.0, 4.0)
    spread = jnp.full((2, 1, 2, 1), D ** (-0.5), jnp.float32)
    spread = spread.at[1, 0, 1, 0].set(max(D // 256, 1) ** (-0.5))
    return (base * spread).astype(jnp.bfloat16)


def draw_norms(key, part):
    key = jax.random.fold_in(key, 14)
    first, second = jax.random.split(key)
    gains = jax.random.uniform(first, (2, 3, 1, D), jnp.float32, 0.6, 1.4)
    shifts = jnp.clip(0.3 * jax.random.normal(second, (2, 3, 1, D), jnp.float32), -1.0, 1.0)
    return jnp.concatenate([gains, shifts], axis=2)


def touch_ends(values, key, smallest, high):
    dims = values.shape
    spot = [jax.random.randint(jax.random.fold_in(key, axis), (), 0, dims[axis]) for axis in range(len(dims))]
    values = values.at[tuple(spot)].set(smallest)
    longest = dims.index(max(dims))
    spot[longest] = (spot[longest] + 1) % dims[longest]
    return values.at[tuple(spot)].set(high)


def block_scale(key, dims, pieces, least, largest):
    def one(axis_at, shards_of):
        draws = jax.random.uniform(jax.random.fold_in(jax.random.fold_in(key, 6), axis_at), (shards_of,), jnp.float32, least / len(pieces), largest / len(pieces))
        return jnp.repeat(jnp.exp(draws), dims[axis_at] // shards_of).reshape((-1,) + (1,) * (len(dims) - axis_at - 1))

    level = one(*pieces[0])
    for cut in pieces[1:]:
        level = level * one(*cut)
    return level


def bell_draw(rng, shape, scale, bound, cuts=(), held_as=jnp.bfloat16):
    loudness = block_scale(rng, shape, cuts, -0.22, 0.18) if cuts else 1.0
    array = jax.random.normal(rng, shape, jnp.float32) * scale * loudness
    return jnp.minimum(jnp.maximum(array, -bound), bound).astype(held_as)


def setup_inputs(seed: int = 0) -> dict:
    key_of = jax.random.split(jax.random.key(seed), 13)
    return {
        "source": bell_draw(key_of[0], (SEQS, SRC, D), 1.0, 6.0, ((0, 4),)),
        "target": bell_draw(key_of[1], (SEQS, TGT, D), 1.0, 6.0, ((0, 4),)),
        "src_len": draw_src_len(jax.random.fold_in(key_of[12], 71), 0),
        "tgt_len": draw_tgt_len(jax.random.fold_in(key_of[12], 71), 0),
        "global_mask": touch_ends((jax.random.randint(key_of[4], (SEQS, SRC), 0, 64) < 1).astype(jnp.int32), jax.random.fold_in(key_of[4], 1), 0, 1),
        "attn_w": bell_draw(key_of[5], (2, D, 3, D), D ** -0.5, 0.21875, ((0, 2), (1, 4), (3, 4))),
        "proj_w": bell_draw(key_of[6], (2, D, D), (max(D // 256, 1)) ** -0.5, 3.5, ((0, 2), (1, 4), (2, 4))),
        "cross_w": draw_cross_w(jax.random.fold_in(key_of[12], 71), 0),
        "up_w": bell_draw(key_of[8], (2, D, FF), D ** -0.5, 0.21875, ((0, 2), (1, 4), (2, 4))),
        "down_w": bell_draw(key_of[9], (2, FF, D), FF ** -0.5, 0.109375, ((0, 2), (1, 4), (2, 4))),
        "norms": draw_norms(jax.random.fold_in(key_of[12], 71), 0),
        "dec_cot": bell_draw(key_of[11], (SEQS, TGT, D), 1.0, 6.0, ((0, 4),)),
    }


@jax.custom_vjp
def low(v):
    return lax.optimization_barrier(v.astype(jnp.bfloat16)).astype(jnp.float32)

@jax.custom_vjp
def low_back(v):
    return v

def low_keep(v):
    return (low(v), None)

def low_pass(kept, grad):
    return (grad,)

def back_keep(v):
    return (v, None)

def back_low(kept, grad):
    return (low(grad),)
low.defvjp(low_keep, low_pass)
low_back.defvjp(back_keep, back_low)
EPS = 1e-05
MASKED = -1000000000.0
HIGHEST = lax.Precision.HIGHEST

def layer_norm(z, gain, shift):
    center = z - lax.optimization_barrier(jnp.mean(z, axis=-1, keepdims=True))
    scaled = center * lax.rsqrt(lax.optimization_barrier(jnp.mean(center * center, axis=-1, keepdims=True)) + EPS)
    return scaled * gain + shift

def project(rows, weight):
    return jnp.einsum('rd,dce->rce', rows, weight, precision=HIGHEST)

def attend(query, keys, values, allowed):
    count = query.shape[0]
    heads = query.shape[1] // HD
    query_heads = query.reshape(count, heads, HD)
    key_heads = keys.reshape(keys.shape[0], heads, HD)
    value_heads = values.reshape(values.shape[0], heads, HD)
    scores = low_back(jnp.einsum('qhd,khd->hqk', query_heads, key_heads, precision=HIGHEST) * HD ** (-0.5))
    scores = jnp.where(allowed[None], scores, MASKED)
    probs = jax.nn.softmax(scores, axis=-1)
    context = jnp.einsum('hqk,khd->qhd', low(probs), value_heads, precision=HIGHEST)
    return context.reshape(count, heads * HD)

def encoder_seq(rows, length, marks, attn_w, proj_w, cross_w, up_w, down_w, norms):
    place = jnp.arange(SRC, dtype=jnp.int32)
    valid = place < length
    marked = marks > 0
    normed = layer_norm(rows, norms[0, 0], norms[0, 1])
    triple = low_back(low(project(low(normed), attn_w)))
    near = jnp.abs(place[:, None] - place[None, :]) <= WINDOW // 2
    allowed = (near | marked[:, None] | marked[None, :]) & valid[None, :]
    context = low_back(low(attend(triple[:, 0], triple[:, 1], triple[:, 2], allowed)))
    mixed = low_back(jnp.dot(context, proj_w, precision=HIGHEST))
    middle = layer_norm(normed + mixed, norms[1, 0], norms[1, 1])
    raised = low_back(jnp.dot(low(middle), up_w, precision=HIGHEST))
    active = low(jax.nn.gelu(raised, approximate=False))
    lowered = low_back(jnp.dot(active, down_w, precision=HIGHEST))
    memory = layer_norm(middle + lowered, norms[2, 0], norms[2, 1]) * valid[:, None]
    return low_back(low(project(low(memory), cross_w)))

def decoder_seq(rows, length, src_length, pairs, attn_w, proj_w, cross_w, up_w, down_w, norms):
    place = jnp.arange(TGT, dtype=jnp.int32)
    valid = place < length
    triple = low_back(low(project(low(rows), attn_w)))
    allowed = (place[None, :] <= place[:, None]) & (place[None, :] < length)
    context = low_back(low(attend(triple[:, 0], triple[:, 1], triple[:, 2], allowed)))
    mixed = low_back(jnp.dot(context, proj_w, precision=HIGHEST))
    first = layer_norm(rows + mixed, norms[0, 0], norms[0, 1])
    asking = low_back(low(jnp.dot(low(first), cross_w[:, 0], precision=HIGHEST)))
    seen = jnp.broadcast_to(jnp.arange(SRC, dtype=jnp.int32)[None, :] < src_length, (TGT, SRC))
    crossed = low_back(low(attend(asking, pairs[:, 0], pairs[:, 1], seen)))
    answer = low_back(jnp.dot(crossed, cross_w[:, 1].T, precision=HIGHEST))
    second = layer_norm(first + answer, norms[1, 0], norms[1, 1])
    raised = low_back(jnp.dot(low(second), up_w, precision=HIGHEST))
    active = low(jax.nn.gelu(raised, approximate=False))
    lowered = low_back(jnp.dot(active, down_w, precision=HIGHEST))
    return layer_norm(second + lowered, norms[2, 0], norms[2, 1]) * valid[:, None]

def reference(source, target, src_len, tgt_len, global_mask, attn_w, proj_w, cross_w, up_w, down_w, norms, dec_cot):

    def forward(src_rows, tgt_rows, attn, proj, cross, upper, downer, gains):

        def encode(item):
            return encoder_seq(item[0], item[1], item[2], attn[0], proj[0], cross[0], upper[0], downer[0], gains[0])
        pairs = lax.map(jax.checkpoint(encode), (src_rows, src_len, global_mask))

        def decode(item):
            return decoder_seq(item[0], item[1], item[2], item[3], attn[1], proj[1], cross[1], upper[1], downer[1], gains[1])
        return lax.map(jax.checkpoint(decode), (tgt_rows, tgt_len, src_len, pairs))
    wide = (source.astype(jnp.float32), target.astype(jnp.float32), attn_w.astype(jnp.float32), proj_w.astype(jnp.float32), cross_w.astype(jnp.float32), up_w.astype(jnp.float32), down_w.astype(jnp.float32), norms.astype(jnp.float32))
    result, pull = jax.vjp(forward, *wide)
    grads = pull(dec_cot.astype(jnp.float32))
    return (result.astype(jnp.bfloat16), grads[0].astype(jnp.bfloat16), grads[1].astype(jnp.bfloat16), grads[2], grads[3], grads[4], grads[5], grads[6], grads[7])
```

```python
import jax
import jax.numpy as jnp
from jax import lax
from jax.experimental import pallas as pl
from jax.experimental.pallas import tpu as pltpu
from jax.sharding import Mesh, PartitionSpec as P

HD = 64
WINDOW = 1024
EPS = 1e-05
MASKED = -1000000000.0
BF = jnp.bfloat16
F32 = jnp.float32
GROUP = 256
EVERY = ("section", "ty", "tc", "dp")


def dot(a, b, ca, cb):
    return lax.dot_general(a, b, (((ca,), (cb,)), ((), ())), preferred_element_type=F32)


def swap(value, axis):
    return lax.ppermute(value, axis, [(0, 1), (1, 0)])


def attend_forward_kernel(q_ref, ko_ref, kp_ref, vo_ref, vp_ref, bias_ref, ctx_ref, wide_ref, lse_ref):
    half = ko_ref.shape[1]
    step = 256
    ones = jnp.ones((16, step), BF)
    for head in range(q_ref.shape[0] // HD):
        feats = pl.ds(head * HD, HD)
        query = q_ref[feats, :]
        pieces = []
        highest = None
        for k_ref, v_ref, base in ((ko_ref, vo_ref, 0), (kp_ref, vp_ref, half)):
            for at in range(0, half, step):
                keys = pl.ds(at, step)
                scores = dot(k_ref[feats, keys], query, 0, 0) + bias_ref[pl.ds(base + at, step), :]
                top = jnp.max(scores, axis=0, keepdims=True)
                highest = top if highest is None else jnp.maximum(highest, top)
                pieces.append((scores, v_ref, keys))
        total = None
        summed = None
        for scores, v_ref, keys in pieces:
            lifted = jnp.exp(scores - highest)
            count = jnp.sum(lifted, axis=0, keepdims=True)
            summed = count if summed is None else summed + count
            part = dot(jnp.concatenate([v_ref[feats, keys], ones], axis=0), lifted.astype(BF), 1, 0)
            total = part if total is None else total + part
        context = total[:HD] / total[HD : HD + 1]
        ctx_ref[feats, :] = context.astype(BF)
        wide_ref[feats, :] = context
        lse_ref[0, head : head + 1, :] = highest + jnp.log(summed)


def attend_forward(q, k_own, k_par, v_own, v_par, bias):
    feats, rows = q.shape
    half = k_own.shape[1]
    groups = feats // GROUP
    block = 256
    side = pl.BlockSpec((GROUP, half), lambda b, g: (g, 0))
    lane = pl.BlockSpec((GROUP, block), lambda b, g: (g, b))
    return pl.pallas_call(
        attend_forward_kernel,
        grid=(rows // block, groups),
        in_specs=[lane, side, side, side, side, pl.BlockSpec((2 * half, block), lambda b, g: (0, b))],
        out_specs=[lane, lane, pl.BlockSpec((1, GROUP // HD, block), lambda b, g: (g, 0, b))],
        out_shape=[
            jax.ShapeDtypeStruct((feats, rows), BF),
            jax.ShapeDtypeStruct((feats, rows), F32),
            jax.ShapeDtypeStruct((groups, GROUP // HD, rows), F32),
        ],
        compiler_params=pltpu.CompilerParams(vmem_limit_bytes=40 * 1024 * 1024),
        cost_estimate=pl.CostEstimate(
            flops=16 * feats * rows * half, bytes_accessed=8 * feats * half, transcendentals=0
        ),
    )(q, k_own, k_par, v_own, v_par, bias)


def attend_backward_kernel(
    q_ref, ko_ref, kp_ref, vo_ref, vp_ref, bias_ref, ctx_ref, lse_ref, do_ref,
    dq_ref, dk_ref, dv_ref, dk_sum, dv_sum,
):
    half = ko_ref.shape[1]
    block = pl.program_id(1)

    @pl.when(block == 0)
    def _():
        dk_sum[...] = jnp.zeros_like(dk_sum)
        dv_sum[...] = jnp.zeros_like(dv_sum)

    for pair in range(q_ref.shape[0] // (2 * HD)):
        wide = pl.ds(pair * 2 * HD, 2 * HD)
        q_rows = q_ref[wide, :].T
        do_rows = do_ref[wide, :].T
        lanes = lax.broadcasted_iota(jnp.int32, q_rows.shape, 1) // HD
        for inner in range(2):
            head = 2 * pair + inner
            feats = pl.ds(head * HD, HD)
            query = q_ref[feats, :]
            grad = do_ref[feats, :]
            q_side = jnp.where(lanes == inner, q_rows, jnp.zeros_like(q_rows))
            do_side = jnp.where(lanes == inner, do_rows, jnp.zeros_like(do_rows))
            lse = lse_ref[0, head : head + 1, :]
            delta = jnp.sum(grad.astype(F32) * ctx_ref[feats, :], axis=0, keepdims=True)
            total = None
            for k_ref, v_ref, base in ((ko_ref, vo_ref, 0), (kp_ref, vp_ref, half)):
                keys = pl.ds(base, half)
                scores = dot(k_ref[feats, :], query, 0, 0) + bias_ref[keys, :]
                probs = jnp.exp(scores - lse)
                grad_probs = dot(v_ref[feats, :], grad, 0, 0)
                grad_scores = (probs * (grad_probs - delta)).astype(BF)
                dv_sum[keys, wide] += dot(probs.astype(BF), do_side, 1, 0)
                dk_sum[keys, wide] += dot(grad_scores, q_side, 1, 0)
                part = dot(k_ref[feats, :], grad_scores, 1, 0)
                total = part if total is None else total + part
            dq_ref[feats, :] = (total * (HD**-0.5)).astype(BF)

    @pl.when(block == pl.num_programs(1) - 1)
    def _():
        dk_ref[...] = dk_sum[...].astype(BF)
        dv_ref[...] = dv_sum[...].astype(BF)


def attend_backward(q, k_own, k_par, v_own, v_par, bias, ctx, lse, grad):
    feats, rows = q.shape
    half = k_own.shape[1]
    groups = feats // GROUP
    block = 256
    side = pl.BlockSpec((GROUP, half), lambda g, b: (g, 0))
    lane = pl.BlockSpec((GROUP, block), lambda g, b: (g, b))
    key_side = pl.BlockSpec((2 * half, GROUP), lambda g, b: (0, g))
    return pl.pallas_call(
        attend_backward_kernel,
        grid=(groups, rows // block),
        in_specs=[
            lane, side, side, side, side,
            pl.BlockSpec((2 * half, block), lambda g, b: (0, b)),
            lane,
            pl.BlockSpec((1, GROUP // HD, block), lambda g, b: (g, 0, b)),
            lane,
        ],
        out_specs=[lane, key_side, key_side],
        out_shape=[
            jax.ShapeDtypeStruct((feats, rows), BF),
            jax.ShapeDtypeStruct((2 * half, feats), BF),
            jax.ShapeDtypeStruct((2 * half, feats), BF),
        ],
        scratch_shapes=[pltpu.VMEM((2 * half, GROUP), F32)] * 2,
        compiler_params=pltpu.CompilerParams(vmem_limit_bytes=48 * 1024 * 1024),
        cost_estimate=pl.CostEstimate(
            flops=40 * feats * rows * half, bytes_accessed=16 * feats * half, transcendentals=0
        ),
    )(q, k_own, k_par, v_own, v_par, bias, ctx, lse, grad)


def layer_norm(z, norm):
    center = z - jnp.mean(z, axis=-1, keepdims=True)
    inverse = lax.rsqrt(jnp.mean(center * center, axis=-1, keepdims=True) + EPS)
    scaled = center * inverse
    return (scaled * norm[0] + norm[1], (scaled, inverse))


def norm_back(grad, kept, norm):
    scaled, inverse = kept
    inner = grad * norm[0]
    back = inverse * (
        inner
        - jnp.mean(inner, axis=-1, keepdims=True)
        - scaled * jnp.mean(inner * scaled, axis=-1, keepdims=True)
    )
    return (back, jnp.stack([jnp.sum(grad * scaled, axis=0), jnp.sum(grad, axis=0)]))


def gelu_both(raised):
    rise = 0.5 * (1.0 + lax.erf(raised * (0.5**0.5)))
    slope = rise + raised * jnp.exp(-0.5 * raised * raised) * 0.3989422804014327
    return ((raised * rise).astype(BF), slope.astype(BF))


def feature_major(weight, rows):
    out = jnp.einsum("tde,rd->ter", weight, rows, preferred_element_type=F32)
    return out.reshape(-1, rows.shape[0])


def heads_major(weight, rows):
    tall = rows.reshape(rows.shape[0], weight.shape[0], weight.shape[2])
    return jnp.einsum("rte,tde->rd", tall, weight, preferred_element_type=F32)


def from_features(weight, feats):
    tall = feats.reshape(weight.shape[0], weight.shape[2], feats.shape[1])
    return jnp.einsum("ter,tde->rd", tall, weight, preferred_element_type=F32)


def local(source, target, src_len, tgt_len, global_mask, attn_w, proj_w, cross_w, up_w, down_w, norms, dec_cot):
    section = lax.axis_index("section")
    y = lax.axis_index("ty")
    c = lax.axis_index("tc")
    src_rows = source.shape[1]
    tgt_rows = target.shape[1]
    width = source.shape[2]
    src_own = src_rows // 4
    tgt_own = tgt_rows // 4
    cut = attn_w.shape[1]
    head_cut = attn_w.shape[3]
    unit_cut = up_w.shape[2]

    def pick(array):
        return lax.dynamic_index_in_dim(array, section, 0, keepdims=False)

    def quarter(array, at_y, at_c):
        size = array.shape[0] // 4
        return lax.dynamic_slice_in_dim(array, (2 * at_y + at_c) * size, size, 0)

    def ordered(array):
        return jnp.concatenate(
            [quarter(array, y, c), quarter(array, 1 - y, c), quarter(array, y, 1 - c), quarter(array, 1 - y, 1 - c)]
        )

    src_length = pick(src_len)
    tgt_length = pick(tgt_len)
    src_place = ordered(jnp.arange(src_rows, dtype=jnp.int32))
    tgt_place = ordered(jnp.arange(tgt_rows, dtype=jnp.int32))
    marks = ordered(pick(global_mask)) > 0
    src_mine = src_place[:src_own]
    tgt_mine = tgt_place[:tgt_own]
    src_valid = (src_mine < src_length).astype(F32)[:, None]
    tgt_valid = (tgt_mine < tgt_length).astype(F32)[:, None]

    def bias_of(allowed):
        return jnp.where(allowed, 0.0, MASKED).astype(F32)

    near = jnp.abs(src_place[:, None] - src_mine[None, :]) <= WINDOW // 2
    enc_bias = bias_of((near | marks[:, None] | marks[None, :src_own]) & (src_place < src_length)[:, None])
    dec_bias = bias_of((tgt_place[:, None] <= tgt_mine[None, :]) & (tgt_place < tgt_length)[:, None])
    cross_bias = bias_of(jnp.broadcast_to((src_place < src_length)[:, None], (src_rows, tgt_own)))

    def gather(shard):
        full = lax.all_gather(shard, EVERY, tiled=True)
        return full.reshape(2, 4, width, shard.shape[1])

    attn_all = gather(jnp.concatenate([attn_w.reshape(cut, 3 * head_cut), proj_w[0].T], axis=1))
    feed_all = gather(jnp.concatenate([up_w.reshape(cut, unit_cut), down_w[0].T], axis=1))
    cross_all = gather(cross_w.reshape(cut, 2 * head_cut))
    norms_all = lax.all_gather(norms, "section", tiled=True)

    def layer(index):
        attn = attn_all[index]
        q = attn[:, :, :head_cut]
        k = attn[:, :, head_cut : 2 * head_cut]
        v = attn[:, :, 2 * head_cut : 3 * head_cut]
        proj = attn[:, :, 3 * head_cut :]
        up = feed_all[index][:, :, :unit_cut]
        down = feed_all[index][:, :, unit_cut:]
        first = cross_all[index][:, :, :head_cut]
        second = cross_all[index][:, :, head_cut:]
        return (q, k, v, proj, up, down, first, second)

    q_e, k_e, v_e, proj_e, up_e, down_e, ck_e, cv_e = layer(0)
    q_d, k_d, v_d, proj_d, up_d, down_d, cq_d, co_d = layer(1)
    norm_e = norms_all[0]
    norm_d = norms_all[1]
    scale = HD**-0.5

    def queries(weight, rows):
        return feature_major(weight, rows).astype(BF) * jnp.asarray(scale, BF)

    def key_values(k_weight, v_weight, rows):
        own = jnp.concatenate([feature_major(k_weight, rows), feature_major(v_weight, rows)]).astype(BF)
        par = swap(own, "tc")
        return (own[:width], par[:width], own[width:], par[width:])

    def feed_forward(low, up, down):
        raised = jnp.einsum("rd,tdu->rtu", low, up, preferred_element_type=F32)
        active, slope = gelu_both(raised)
        return (active, slope, jnp.einsum("rtu,tdu->rd", active, down, preferred_element_type=F32))

    def feed_back(low, active, slope, lowered_grad, up, down):
        grad_active = jnp.einsum("rd,tdu->rtu", lowered_grad, down, preferred_element_type=F32)
        raised_grad = (grad_active * slope.astype(F32)).astype(BF)
        grad_down = jnp.einsum("rd,rtu->tdu", lowered_grad, active, preferred_element_type=F32)
        grad_up = jnp.einsum("rd,rtu->tdu", low, raised_grad, preferred_element_type=F32)
        back = jnp.einsum("rtu,tdu->rd", raised_grad, up, preferred_element_type=F32)
        return (back, grad_up, grad_down)

    def split(rows):
        return rows.reshape(rows.shape[0], 4, rows.shape[1] // 4)

    def split_feats(feats):
        return feats.reshape(4, feats.shape[0] // 4, feats.shape[1])

    def chip_sum(dk, dv):
        half = dk.shape[0] // 2
        other = swap(jnp.concatenate([dk[half:], dv[half:]], axis=1), "tc")
        own = jnp.concatenate([dk[:half], dv[:half]], axis=1)
        total = (own.astype(F32) + other.astype(F32)).astype(BF)
        return (total[:, :width], total[:, width:])

    def chip_rows(k_weight, v_weight, dk, dv):
        partial_rows = heads_major(k_weight, dk) + heads_major(v_weight, dv)
        mine = partial_rows.shape[0] // 2
        return (partial_rows[:mine], swap(partial_rows[mine:].astype(BF), "ty").astype(F32))

    src = pick(source)
    src_set = jnp.concatenate([quarter(src, y, c), quarter(src, 1 - y, c)]).astype(F32)
    normed, kept = layer_norm(src_set, norm_e[0])
    enc_kept_zero = (kept[0][:src_own], kept[1][:src_own])
    normed_low = normed.astype(BF)
    normed_mine = normed[:src_own]
    low_mine = normed_low[:src_own]
    enc_q = queries(q_e, low_mine)
    enc_kv = key_values(k_e, v_e, normed_low)
    enc_ctx, enc_wide, enc_lse = attend_forward(enc_q, *enc_kv, enc_bias)
    middle, enc_kept_one = layer_norm(normed_mine + from_features(proj_e, enc_ctx), norm_e[1])
    middle_low = middle.astype(BF)
    enc_active, enc_slope, lowered = feed_forward(middle_low, up_e, down_e)
    memory, enc_kept_two = layer_norm(middle + lowered, norm_e[2])
    memory_low = (memory * src_valid).astype(BF)
    memory_set = jnp.concatenate([memory_low, swap(memory_low, "ty")])
    mem_kv = key_values(ck_e, cv_e, memory_set)

    tgt = pick(target)
    tgt_set = jnp.concatenate([quarter(tgt, y, c), quarter(tgt, 1 - y, c)])
    tgt_low = tgt_set[:tgt_own]
    dec_q = queries(q_d, tgt_low)
    dec_kv = key_values(k_d, v_d, tgt_set)
    dec_ctx, dec_wide, dec_lse = attend_forward(dec_q, *dec_kv, dec_bias)
    first, dec_kept_zero = layer_norm(tgt_low.astype(F32) + from_features(proj_d, dec_ctx), norm_d[0])
    first_low = first.astype(BF)
    asking = queries(cq_d, first_low)
    crossed, cross_wide, cross_lse = attend_forward(asking, *mem_kv, cross_bias)
    second, dec_kept_one = layer_norm(first + from_features(co_d, crossed), norm_d[1])
    second_low = second.astype(BF)
    dec_active, dec_slope, lowered = feed_forward(second_low, up_d, down_d)
    result, dec_kept_two = layer_norm(second + lowered, norm_d[2])
    output = (result * tgt_valid).astype(BF)

    cotangent = quarter(pick(dec_cot), y, c).astype(F32) * tgt_valid
    back_two, dnorm_d2 = norm_back(cotangent, dec_kept_two, norm_d[2])
    lowered_grad = back_two.astype(BF)
    back, grad_up_d, grad_down_d = feed_back(second_low, dec_active, dec_slope, lowered_grad, up_d, down_d)
    back_one, dnorm_d1 = norm_back(back_two + back, dec_kept_one, norm_d[1])
    answer_grad = back_one.astype(BF)
    grad_co = jnp.einsum("rd,ter->tde", answer_grad, split_feats(crossed), preferred_element_type=F32)
    crossed_grad = feature_major(co_d, answer_grad).astype(BF)
    asking_grad, mem_dk, mem_dv = attend_backward(asking, *mem_kv, cross_bias, cross_wide, cross_lse, crossed_grad)
    mem_dk, mem_dv = chip_sum(mem_dk, mem_dv)
    grad_cq = jnp.einsum("rd,ter->tde", first_low, split_feats(asking_grad), preferred_element_type=F32)
    back_zero, dnorm_d0 = norm_back(back_one + from_features(cq_d, asking_grad), dec_kept_zero, norm_d[0])
    mixed_grad = back_zero.astype(BF)
    grad_proj_d = jnp.einsum("rd,ter->tde", mixed_grad, split_feats(dec_ctx), preferred_element_type=F32)
    ctx_grad = feature_major(proj_d, mixed_grad).astype(BF)
    dq, dk, dv = attend_backward(dec_q, *dec_kv, dec_bias, dec_wide, dec_lse, ctx_grad)
    dk, dv = chip_sum(dk, dv)
    grad_attn_d = jnp.concatenate(
        [
            jnp.einsum("rd,ter->tde", tgt_low, split_feats(dq), preferred_element_type=F32),
            jnp.einsum("rd,rte->tde", tgt_set, split(dk), preferred_element_type=F32),
            jnp.einsum("rd,rte->tde", tgt_set, split(dv), preferred_element_type=F32),
        ],
        axis=2,
    )
    mine, other = chip_rows(k_d, v_d, dk, dv)
    target_grad = (back_zero + mine + other + from_features(q_d, dq)).astype(BF)

    grad_cross_e = jnp.concatenate(
        [
            jnp.einsum("rd,rte->tde", memory_set, split(mem_dk), preferred_element_type=F32),
            jnp.einsum("rd,rte->tde", memory_set, split(mem_dv), preferred_element_type=F32),
        ],
        axis=2,
    )
    mine, other = chip_rows(ck_e, cv_e, mem_dk, mem_dv)
    back_two, dnorm_e2 = norm_back((mine + other) * src_valid, enc_kept_two, norm_e[2])
    lowered_grad = back_two.astype(BF)
    back, grad_up_e, grad_down_e = feed_back(middle_low, enc_active, enc_slope, lowered_grad, up_e, down_e)
    back_one, dnorm_e1 = norm_back(back_two + back, enc_kept_one, norm_e[1])
    mixed_grad = back_one.astype(BF)
    grad_proj_e = jnp.einsum("rd,ter->tde", mixed_grad, split_feats(enc_ctx), preferred_element_type=F32)
    ctx_grad = feature_major(proj_e, mixed_grad).astype(BF)
    dq, dk, dv = attend_backward(enc_q, *enc_kv, enc_bias, enc_wide, enc_lse, ctx_grad)
    dk, dv = chip_sum(dk, dv)
    grad_attn_e = jnp.concatenate(
        [
            jnp.einsum("rd,ter->tde", low_mine, split_feats(dq), preferred_element_type=F32),
            jnp.einsum("rd,rte->tde", normed_low, split(dk), preferred_element_type=F32),
            jnp.einsum("rd,rte->tde", normed_low, split(dv), preferred_element_type=F32),
        ],
        axis=2,
    )
    mine, other = chip_rows(k_e, v_e, dk, dv)
    back_zero, dnorm_e0 = norm_back(back_one + mine + other + from_features(q_e, dq), enc_kept_zero, norm_e[0])
    source_grad = back_zero.astype(BF)

    def scatter(enc, dec):
        both = jnp.stack([enc, dec]).astype(BF).reshape(-1, enc.shape[2])
        return lax.psum_scatter(both, EVERY, tiled=True).astype(F32)

    attn_sum = scatter(
        jnp.concatenate([grad_attn_e, grad_proj_e], axis=2), jnp.concatenate([grad_attn_d, grad_proj_d], axis=2)
    )
    feed_sum = scatter(
        jnp.concatenate([grad_up_e, grad_down_e], axis=2), jnp.concatenate([grad_up_d, grad_down_d], axis=2)
    )
    cross_sum = scatter(grad_cross_e, jnp.concatenate([grad_cq, grad_co], axis=2))
    norm_sum = lax.psum(
        jnp.stack([jnp.stack([dnorm_e0, dnorm_e1, dnorm_e2]), jnp.stack([dnorm_d0, dnorm_d1, dnorm_d2])]), EVERY
    )
    norm_share = lax.dynamic_slice(
        norm_sum, (section, 0, 0, lax.axis_index("dp") * cut), (1, 3, 2, cut)
    )

    def everyone(rows):
        full = lax.all_gather(rows, ("section", "ty", "tc"), tiled=True)
        return full.reshape(2, -1, width)

    return (
        everyone(output),
        everyone(source_grad),
        everyone(target_grad),
        attn_sum[:, : 3 * head_cut].reshape(1, cut, 3, head_cut),
        attn_sum[:, 3 * head_cut :].T[None],
        cross_sum.reshape(1, cut, 2, head_cut),
        feed_sum[None, :, :unit_cut],
        feed_sum[:, unit_cut:].T[None],
        norm_share,
    )


def solution(mesh):
    shape = mesh.devices.shape
    fine = Mesh(mesh.devices.reshape(shape[0], shape[1], 2, 2), ("section", "dp", "ty", "tc"))
    tensor = ("ty", "tc")
    return jax.shard_map(
        local,
        mesh=fine,
        in_specs=(
            P("dp", None, None),
            P("dp", None, None),
            P("dp"),
            P("dp"),
            P("dp", None),
            P("section", "dp", None, tensor),
            P("section", tensor, "dp"),
            P("section", "dp", None, tensor),
            P("section", "dp", tensor),
            P("section", tensor, "dp"),
            P("section", None, None, None),
            P("dp", None, None),
        ),
        out_specs=(
            P("dp", None, None),
            P("dp", None, None),
            P("dp", None, None),
            P("section", "dp", None, tensor),
            P("section", tensor, "dp"),
            P("section", "dp", None, tensor),
            P("section", "dp", tensor),
            P("section", tensor, "dp"),
            P("section", None, None, "dp"),
        ),
        check_vma=False,
    )
```

```python
import functools

import jax
import jax.numpy as jnp
from jax import lax
from jax.experimental import pallas as pl
from jax.experimental.pallas import tpu as pltpu
from jax.sharding import Mesh, PartitionSpec as P

HD = 64
WINDOW = 1024
EPS = 1e-05
MASKED = -1000000000.0
BF = jnp.bfloat16
F32 = jnp.float32
BLOCK = 256


def dot(a, b, ca, cb):
    return lax.dot_general(a, b, (((ca,), (cb,)), ((), ())), preferred_element_type=F32)


def fill_bias(mode, seg, place_ref, key_bias_ref, key_mark_ref, q_mark_ref, bias_ref):
    lanes = bias_ref.shape[1]
    for at in range(0, bias_ref.shape[0], seg):
        keys = pl.ds(at, seg)
        key_bias = key_bias_ref[keys, :]
        if mode == "all":
            bias_ref[keys, :] = jnp.broadcast_to(key_bias, (seg, lanes))
            continue
        key_place = place_ref[at // seg] + lax.broadcasted_iota(jnp.int32, (seg, lanes), 0)
        query_place = place_ref[4 + pl.program_id(0)] + lax.broadcasted_iota(jnp.int32, (seg, lanes), 1)
        if mode == "causal":
            allowed = key_place <= query_place
        else:
            allowed = (jnp.abs(key_place - query_place) <= WINDOW // 2) | (key_mark_ref[keys, :] + q_mark_ref[...] > 0.5)
        bias_ref[keys, :] = jnp.where(allowed, key_bias, MASKED)


def attend_forward_kernel(mode, chunks, place_ref, *refs):
    q_refs = refs[:chunks]
    near_refs = refs[chunks : 2 * chunks]
    far_refs = refs[2 * chunks : 3 * chunks]
    key_bias_ref, key_mark_ref, q_mark_ref = refs[3 * chunks : 3 * chunks + 3]
    outs = refs[3 * chunks + 3 :]
    ctx_refs, wide_refs, lse_ref, bias_ref = outs[:chunks], outs[chunks : 2 * chunks], outs[2 * chunks], outs[-1]
    cut = q_refs[0].shape[0]
    half = near_refs[0].shape[1]
    step = 256
    ones = jnp.ones((16, step), BF)
    fill_bias(mode, half // 2, place_ref, key_bias_ref, key_mark_ref, q_mark_ref, bias_ref)
    for chunk in range(chunks):
        for inner in range(cut // HD):
            feats = pl.ds(inner * HD, HD)
            value_feats = pl.ds(cut + inner * HD, HD)
            query = q_refs[chunk][feats, :]
            pieces = []
            highest = None
            for kv_ref, base in ((near_refs[chunk], 0), (far_refs[chunk], half)):
                for at in range(0, half, step):
                    keys = pl.ds(at, step)
                    scores = dot(kv_ref[feats, keys], query, 0, 0) + bias_ref[pl.ds(base + at, step), :]
                    top = jnp.max(scores, axis=0, keepdims=True)
                    highest = top if highest is None else jnp.maximum(highest, top)
                    pieces.append((scores, kv_ref, keys))
            total = None
            summed = None
            for scores, kv_ref, keys in pieces:
                lifted = jnp.exp(scores - highest)
                count = jnp.sum(lifted, axis=0, keepdims=True)
                summed = count if summed is None else summed + count
                value = jnp.concatenate([kv_ref[value_feats, keys], ones], axis=0)
                part = dot(value, lifted.astype(BF), 1, 0)
                total = part if total is None else total + part
            context = total[:HD] / total[HD : HD + 1]
            ctx_refs[chunk][feats, :] = context.astype(BF)
            wide_refs[chunk][feats, :] = context
            head = chunk * (cut // HD) + inner
            lse_ref[head : head + 1, :] = highest + jnp.log(summed)


def mask_specs(half):
    return [
        pl.BlockSpec((2 * half, 1), lambda b, p: (0, 0)),
        pl.BlockSpec((2 * half, 1), lambda b, p: (0, 0)),
        pl.BlockSpec((1, BLOCK), lambda b, p: (0, b)),
    ]


def attend_forward(mode, q, near, far, mask):
    chunks = len(q)
    cut, rows = q[0].shape
    half = near[0].shape[1]
    heads = chunks * cut // HD
    side = pl.BlockSpec((2 * cut, half), lambda b, p: (0, 0))
    lane = pl.BlockSpec((cut, BLOCK), lambda b, p: (0, b))
    out = pl.pallas_call(
        functools.partial(attend_forward_kernel, mode, chunks),
        grid_spec=pltpu.PrefetchScalarGridSpec(
            num_scalar_prefetch=1,
            grid=(rows // BLOCK,),
            in_specs=[lane] * chunks + [side] * (2 * chunks) + mask_specs(half),
            out_specs=[lane] * (2 * chunks) + [pl.BlockSpec((heads, BLOCK), lambda b, p: (0, b))],
            scratch_shapes=[pltpu.VMEM((2 * half, BLOCK), F32)],
        ),
        out_shape=[jax.ShapeDtypeStruct((cut, rows), BF)] * chunks
        + [jax.ShapeDtypeStruct((cut, rows), F32)] * chunks
        + [jax.ShapeDtypeStruct((heads, rows), F32)],
        compiler_params=pltpu.CompilerParams(vmem_limit_bytes=48 * 1024 * 1024),
        cost_estimate=pl.CostEstimate(
            flops=32 * chunks * cut * rows * half, bytes_accessed=8 * chunks * cut * half, transcendentals=0
        ),
    )(mask[0], *q, *near, *far, *mask[1:])
    return (out[:chunks], out[chunks : 2 * chunks], out[2 * chunks])


def attend_backward_kernel(mode, chunks, place_ref, *refs):
    q_refs = refs[:chunks]
    near_refs = refs[chunks : 2 * chunks]
    far_refs = refs[2 * chunks : 3 * chunks]
    key_bias_ref, key_mark_ref, q_mark_ref = refs[3 * chunks : 3 * chunks + 3]
    rest = refs[3 * chunks + 3 :]
    wide_refs, lse_ref, do_refs = rest[:chunks], rest[chunks], rest[chunks + 1 : 2 * chunks + 1]
    outs = rest[2 * chunks + 1 :]
    dq_refs, dkv_refs, sums, bias_ref = outs[:chunks], outs[chunks : 2 * chunks], outs[2 * chunks : 3 * chunks], outs[-1]
    cut = q_refs[0].shape[0]
    heads = cut // HD
    half = near_refs[0].shape[1]
    block = pl.program_id(0)
    fill_bias(mode, half // 2, place_ref, key_bias_ref, key_mark_ref, q_mark_ref, bias_ref)

    @pl.when(block == 0)
    def _():
        for total in sums:
            total[...] = jnp.zeros_like(total)

    def placed(feats, slot):
        blank = jnp.zeros_like(feats)
        pair = [feats, blank] if slot % 2 == 0 else [blank, feats]
        return jnp.concatenate(pair, axis=0).T

    for chunk in range(chunks):
        for inner in range(heads):
            feats = pl.ds(inner * HD, HD)
            value_feats = pl.ds(cut + inner * HD, HD)
            query = q_refs[chunk][feats, :]
            grad = do_refs[chunk][feats, :]
            q_side = placed(query, inner)
            do_side = placed(grad, heads + inner)
            key_lanes = pl.ds(inner // 2 * 2 * HD, 2 * HD)
            value_lanes = pl.ds((heads + inner) // 2 * 2 * HD, 2 * HD)
            head = chunk * heads + inner
            lse = lse_ref[head : head + 1, :]
            delta = jnp.sum(grad.astype(F32) * wide_refs[chunk][feats, :], axis=0, keepdims=True)
            total = None
            for kv_ref, base in ((near_refs[chunk], 0), (far_refs[chunk], half)):
                keys = pl.ds(base, half)
                scores = dot(kv_ref[feats, :], query, 0, 0) + bias_ref[keys, :]
                probs = jnp.exp(scores - lse)
                grad_probs = dot(kv_ref[value_feats, :], grad, 0, 0)
                grad_scores = (probs * (grad_probs - delta)).astype(BF)
                sums[chunk][keys, value_lanes] += dot(probs.astype(BF), do_side, 1, 0)
                sums[chunk][keys, key_lanes] += dot(grad_scores, q_side, 1, 0)
                part = dot(kv_ref[feats, :], grad_scores, 1, 0)
                total = part if total is None else total + part
            dq_refs[chunk][feats, :] = (total * (HD**-0.5)).astype(BF)

    @pl.when(block == pl.num_programs(0) - 1)
    def _():
        for chunk in range(chunks):
            dkv_refs[chunk][...] = sums[chunk][...].astype(BF)


def attend_backward(mode, q, near, far, mask, wide, lse, grad):
    chunks = len(q)
    cut, rows = q[0].shape
    half = near[0].shape[1]
    heads = chunks * cut // HD
    side = pl.BlockSpec((2 * cut, half), lambda b, p: (0, 0))
    lane = pl.BlockSpec((cut, BLOCK), lambda b, p: (0, b))
    key_side = pl.BlockSpec((2 * half, 2 * cut), lambda b, p: (0, 0))
    out = pl.pallas_call(
        functools.partial(attend_backward_kernel, mode, chunks),
        grid_spec=pltpu.PrefetchScalarGridSpec(
            num_scalar_prefetch=1,
            grid=(rows // BLOCK,),
            in_specs=[lane] * chunks
            + [side] * (2 * chunks)
            + mask_specs(half)
            + [lane] * chunks
            + [pl.BlockSpec((heads, BLOCK), lambda b, p: (0, b))]
            + [lane] * chunks,
            out_specs=[lane] * chunks + [key_side] * chunks,
            scratch_shapes=[pltpu.VMEM((2 * half, 2 * cut), F32)] * chunks + [pltpu.VMEM((2 * half, BLOCK), F32)],
        ),
        out_shape=[jax.ShapeDtypeStruct((cut, rows), BF)] * chunks
        + [jax.ShapeDtypeStruct((2 * half, 2 * cut), BF)] * chunks,
        compiler_params=pltpu.CompilerParams(vmem_limit_bytes=56 * 1024 * 1024),
        cost_estimate=pl.CostEstimate(
            flops=80 * chunks * cut * rows * half, bytes_accessed=16 * chunks * cut * half, transcendentals=0
        ),
    )(mask[0], *q, *near, *far, *mask[1:], *wide, lse, *grad)
    return (out[:chunks], out[chunks:])


def assemble_kernel(widths, at_ref, *refs):
    step = pl.program_id(0)
    slots, outs = refs[:4], refs[4:]
    for index in range(4):

        @pl.when(step == index)
        def _():
            start = 0
            for width, out in zip(widths, outs):
                out[...] = slots[index][:, start : start + width]
                start += width


def assemble(at, slots, widths):
    rows, columns = slots[0].shape
    return pl.pallas_call(
        functools.partial(assemble_kernel, widths),
        grid_spec=pltpu.PrefetchScalarGridSpec(
            num_scalar_prefetch=1,
            grid=(4,),
            in_specs=[pl.BlockSpec((rows, columns), lambda k, at: (0, 0))] * 4,
            out_specs=[pl.BlockSpec((rows, width), lambda k, at: ((at[0] + k) % 4, 0)) for width in widths],
        ),
        out_shape=[jax.ShapeDtypeStruct((4 * rows, width), BF) for width in widths],
        compiler_params=pltpu.CompilerParams(vmem_limit_bytes=40 * 1024 * 1024),
    )(at.reshape(1), *slots)


def layer_norm(z, norm):
    center = z - jnp.mean(z, axis=-1, keepdims=True)
    inverse = lax.rsqrt(jnp.mean(center * center, axis=-1, keepdims=True) + EPS)
    scaled = center * inverse
    return (scaled * norm[0] + norm[1], (scaled, inverse))


def norm_back(grad, kept, norm):
    scaled, inverse = kept
    inner = grad * norm[0]
    back = inverse * (
        inner
        - jnp.mean(inner, axis=-1, keepdims=True)
        - scaled * jnp.mean(inner * scaled, axis=-1, keepdims=True)
    )
    return (back, jnp.stack([jnp.sum(grad * scaled, axis=0), jnp.sum(grad, axis=0)]))


def gelu_both(raised):
    rise = 0.5 * (1.0 + lax.erf(raised * (0.5**0.5)))
    slope = rise + raised * jnp.exp(-0.5 * raised * raised) * 0.3989422804014327
    return ((raised * rise).astype(BF), slope.astype(BF))


def hop(value, axis, pairs):
    return lax.ppermute(value, axis, pairs)


def swap(value, axis):
    return hop(value, axis, [(0, 1), (1, 0)])


def crossing(value, to):
    pairs = [(2 * (1 - to) + y, 2 * to + 1 - y) for y in range(2)]
    return hop(value, ("section", "ty"), pairs)


def cut_gather(shard, widths, quick):
    if lax.axis_size("dp") != 4 or not quick:
        full = lax.all_gather(shard, "dp", tiled=True)
        edges = [sum(widths[:i]) for i in range(1, len(widths))]
        return jnp.split(full, edges, axis=1)
    at = lax.axis_index("dp")
    up = hop(shard, "dp", [(j, (j - 1) % 4) for j in range(4)])
    down = hop(shard, "dp", [(j, (j + 1) % 4) for j in range(4)])
    from_up = hop(up, "dp", [(1, 0), (2, 1)])
    from_down = hop(down, "dp", [(1, 2), (2, 3)])
    far = jnp.where(at < 2, from_up, from_down)
    return assemble(at, (shard, up, far, down), widths)


def cut_scatter(tensors, quick):
    size = lax.axis_size("dp")
    if size != 4 or not quick:
        full = jnp.concatenate(tensors, axis=1)
        return lax.psum_scatter(full, "dp", tiled=True).astype(F32)
    at = lax.axis_index("dp")
    rows = tensors[0].shape[0] // 4

    def slot(k):
        start = lax.rem(at + k, 4) * rows
        return jnp.concatenate([lax.dynamic_slice_in_dim(t, start, rows, 0) for t in tensors], axis=1)

    far = slot(2)
    to_up = hop(far, "dp", [(0, 1), (1, 2)])
    to_down = hop(far, "dp", [(2, 1), (3, 2)])
    ahead = add_low(slot(1), to_up)
    behind = add_low(slot(3), to_down)
    from_behind = hop(ahead, "dp", [(j, (j + 1) % 4) for j in range(4)])
    from_ahead = hop(behind, "dp", [(j, (j - 1) % 4) for j in range(4)])
    return slot(0).astype(F32) + from_behind.astype(F32) + from_ahead.astype(F32)


def add_low(a, b):
    return (a.astype(F32) + b.astype(F32)).astype(BF)


def everywhere(value):
    for axis in ("tc", "ty", "section"):
        value = value + swap(value, axis)
    size = lax.axis_size("dp")
    reach = 1
    while reach < size:
        value = value + hop(value, "dp", [(j, j ^ reach) for j in range(size)])
        reach *= 2
    return value


def tie(value, token):
    first = token[(0,) * token.ndim]
    return jnp.where(first == first, value, jnp.zeros_like(value))


def total_of(parts):
    total = parts[0]
    for part in parts[1:]:
        total = total + part
    return total


def local(source, target, src_len, tgt_len, global_mask, attn_w, proj_w, cross_w, up_w, down_w, norms, dec_cot):
    section = lax.axis_index("section")
    y = lax.axis_index("ty")
    c = lax.axis_index("tc")
    src_rows = source.shape[1]
    tgt_rows = target.shape[1]
    width = source.shape[2]
    src_own = src_rows // 4
    tgt_own = tgt_rows // 4
    cut = attn_w.shape[1]
    heads = attn_w.shape[3]
    units = up_w.shape[2]
    scale = HD**-0.5

    def pick(array):
        return lax.dynamic_index_in_dim(array, section, 0, keepdims=False)

    src_length = pick(src_len)
    tgt_length = pick(tgt_len)
    order = jnp.stack([2 * y + c, 2 * y + 1 - c, 2 * (1 - y) + c, 2 * (1 - y) + 1 - c]).astype(jnp.int32)

    def ordered(array):
        size = array.shape[0] // 4
        return jnp.concatenate([lax.dynamic_slice_in_dim(array, order[i] * size, size, 0) for i in range(4)])

    src_place = ordered(jnp.arange(src_rows, dtype=jnp.int32))
    tgt_place = ordered(jnp.arange(tgt_rows, dtype=jnp.int32))
    src_valid = (src_place[:src_own] < src_length).astype(F32)[:, None]
    tgt_valid = (tgt_place[:tgt_own] < tgt_length).astype(F32)[:, None]
    marks = ordered(pick(global_mask) > 0).astype(F32)
    src_bias = jnp.where(src_place < src_length, 0.0, MASKED).astype(F32)[:, None]
    tgt_bias = jnp.where(tgt_place < tgt_length, 0.0, MASKED).astype(F32)[:, None]

    def places(place, queries):
        size = place.shape[0] // 4
        return jnp.concatenate([place[::size], queries[::BLOCK]])

    src_chip = 2 * src_own
    tgt_chip = 2 * tgt_own
    enc_mask = (places(src_place, src_place[:src_chip]), src_bias, marks[:, None], marks[None, :src_chip])
    dec_mask = (places(tgt_place, tgt_place[:tgt_chip]), tgt_bias, tgt_bias, tgt_bias[:tgt_chip].T)
    cross_mask = (places(src_place, tgt_place[:tgt_chip]), src_bias, src_bias, dec_mask[3])

    flat = attn_w.reshape(cut, 3 * heads)
    kv_cut = flat[:, heads:]
    qp_cut = jnp.concatenate([flat[:, :heads], proj_w[0].T], axis=1)
    up_cut = up_w.reshape(cut, units)
    down_cut = down_w[0].T
    cross_cut = cross_w.reshape(cut, 2 * heads)

    cuts = {"kv": kv_cut, "qp": qp_cut, "up": up_cut, "down": down_cut, "cross": cross_cut}
    sizes = {name: value.shape[1] for name, value in cuts.items()}

    def packed(names):
        return jnp.concatenate([cuts[name] for name in names], axis=1)

    def spread(layer, names, full):
        chunks = {}
        for name, mine in zip(names, full):
            by_x = name in ("kv", "up") or (name == "cross" and layer == 0)
            chunks[name] = [mine, swap(mine, "section" if by_x else "ty")]
        return chunks

    norms_all = jnp.stack([norms[0], swap(norms[0], "section")])
    norms_all = jnp.where(section == 0, norms_all, norms_all[::-1])
    norm_e = norms_all[0]
    norm_d = norms_all[1]

    attn_names, feed_names = ("kv", "qp"), ("up", "down")
    attn_width = sizes["kv"] + sizes["qp"]
    feed_width = sizes["up"] + sizes["down"]
    everything = packed(attn_names + feed_names + ("cross",))
    came = hop(everything, ("section", "ty"), [(2 * x + v, 2 * (1 - x) + 1 - v) for x in range(2) for v in range(2)])
    all_e = jnp.where(section == 0, everything, came)
    all_d = jnp.where(section == 1, everything, came)

    full = cut_gather(all_e[:, :attn_width], [sizes[name] for name in attn_names], True)
    w_e = spread(0, attn_names, full)
    shard = all_e[:, attn_width : attn_width + feed_width]
    w_e.update(spread(0, feed_names, cut_gather(shard, [sizes[name] for name in feed_names], False)))
    token = w_e["up"][0]
    shard = jnp.concatenate([all_e[:, attn_width + feed_width :], all_d[:, :attn_width]], axis=1)
    full = cut_gather(tie(shard, token), [sizes["cross"], sizes["kv"], sizes["qp"]], False)
    w_e.update(spread(0, ("cross",), full[:1]))
    w_d = spread(1, attn_names, full[1:])
    token = w_d["kv"][0]
    names = ("cross",) + feed_names
    shard = jnp.concatenate([all_d[:, attn_width + feed_width :], all_d[:, attn_width : attn_width + feed_width]], axis=1)
    w_d.update(spread(1, names, cut_gather(tie(shard, token), [sizes[name] for name in names], False)))

    both = range(2)

    def key_values(weights, rows):
        return [dot(weights[r], rows, 0, 1).astype(BF) for r in both]

    def queries(weights, rows):
        return [(dot(weights[r][:, :heads], rows, 0, 1) * scale).astype(BF) for r in both]

    def chip(rows):
        return jnp.concatenate([rows, swap(rows, "tc")])

    def own_sum(partial_rows):
        mine = partial_rows.shape[0] // 2
        return partial_rows[:mine] + swap(partial_rows[mine:].astype(BF), "tc").astype(F32)

    def feed_forward(low, up, down):
        active, slope, parts = [], [], []
        for r in both:
            act, rise = gelu_both(dot(low, up[r], 1, 0))
            active.append(act)
            slope.append(rise)
            parts.append(dot(act, down[r], 1, 1))
        return (active, slope, own_sum(total_of(parts)))

    def chip_total(partial_of, by_x):
        other = swap(partial_of(1).astype(BF), "section" if by_x else "ty")

        def finish(token):
            return (partial_of(0) + tie(other, token).astype(F32)).astype(BF)

        return finish

    def feed_back(low, active, slope, lowered_grad, up, down):
        raised = []
        for r in both:
            grad_active = dot(lowered_grad, down[r], 1, 0)
            raised.append((grad_active * slope[r].astype(F32)).astype(BF))
        back = own_sum(total_of([dot(raised[r], up[r], 1, 1) for r in both]))
        grad_up = chip_total(lambda r: dot(low, raised[r], 0, 0), True)
        grad_down = chip_total(lambda r: dot(lowered_grad, active[r], 0, 0), False)
        return (back, grad_up, grad_down)

    def project(ctx, weights, start):
        return total_of([dot(ctx[r], weights[r][:, start : start + heads], 0, 1) for r in both])

    def project_back(rows, weights, start):
        return [dot(weights[r][:, start : start + heads], rows, 0, 1).astype(BF) for r in both]

    def all_rows(weights, grads, more):
        partial_rows = total_of([dot(grads[r], weights[r], 1, 1) for r in both])
        size = partial_rows.shape[0] // 4
        parts = [partial_rows[i * size : (i + 1) * size] for i in range(4)]
        if more is not None:
            parts = [parts[0] + more[:size], parts[1] + more[size:], parts[2], parts[3]]
        from_core = swap(jnp.concatenate([parts[1], parts[3]]).astype(BF), "tc").astype(F32)
        leaving = (parts[2] + from_core[size:]).astype(BF)
        return (parts[0] + from_core[:size], swap(leaving, "ty"), leaving)

    normed, kept = layer_norm(ordered(pick(source)).astype(F32), norm_e[0])
    enc_kept_zero = (kept[0][:src_own], kept[1][:src_own])
    normed_low = normed.astype(BF)
    normed_mine = normed[:src_own]
    low_chip = normed_low[:src_chip]
    enc_near = key_values(w_e["kv"], low_chip)
    enc_far = key_values(w_e["kv"], normed_low[src_chip:])
    enc_q = queries(w_e["qp"], low_chip)
    enc_ctx, enc_wide, enc_lse = attend_forward("window", enc_q, enc_near, enc_far, enc_mask)
    middle, enc_kept_one = layer_norm(normed_mine + own_sum(project(enc_ctx, w_e["qp"], heads)), norm_e[1])
    middle_low = chip(middle.astype(BF))
    enc_active, enc_slope, lowered = feed_forward(middle_low, w_e["up"], w_e["down"])
    memory, enc_kept_two = layer_norm(middle + lowered, norm_e[2])
    memory_low = (memory * src_valid).astype(BF)
    memory_near = chip(memory_low)
    memory_far = chip(swap(memory_low, "ty"))
    mem_near = key_values(w_e["cross"], memory_near)
    mem_far = key_values(w_e["cross"], memory_far)

    tgt_low = ordered(pick(target))
    tgt_low_chip = tgt_low[:tgt_chip]
    dec_near = key_values(w_d["kv"], tgt_low_chip)
    dec_far = key_values(w_d["kv"], tgt_low[tgt_chip:])
    dec_q = queries(w_d["qp"], tgt_low_chip)
    dec_ctx, dec_wide, dec_lse = attend_forward("causal", dec_q, dec_near, dec_far, dec_mask)
    first, dec_kept_zero = layer_norm(
        tgt_low[:tgt_own].astype(F32) + own_sum(project(dec_ctx, w_d["qp"], heads)), norm_d[0]
    )
    first_low = chip(first.astype(BF))
    asking = queries(w_d["cross"], first_low)
    mem_near, mem_far = (mem_near[::-1], mem_far[::-1])
    crossed, cross_wide, cross_lse = attend_forward("all", asking, mem_near, mem_far, cross_mask)
    second, dec_kept_one = layer_norm(first + own_sum(project(crossed, w_d["cross"], heads)), norm_d[1])
    second_low = chip(second.astype(BF))
    dec_active, dec_slope, lowered = feed_forward(second_low, w_d["up"], w_d["down"])
    result, dec_kept_two = layer_norm(second + lowered, norm_d[2])
    output = (result * tgt_valid).astype(BF)

    cotangent = lax.dynamic_slice_in_dim(pick(dec_cot), order[0] * tgt_own, tgt_own, 0).astype(F32) * tgt_valid
    back_two, dnorm_d2 = norm_back(cotangent, dec_kept_two, norm_d[2])
    back, grad_up_d, grad_down_d = feed_back(
        second_low, dec_active, dec_slope, chip(back_two.astype(BF)), w_d["up"], w_d["down"]
    )
    back_one, dnorm_d1 = norm_back(back_two + back, dec_kept_one, norm_d[1])
    answer_grad = chip(back_one.astype(BF))
    crossed_grad = project_back(answer_grad, w_d["cross"], heads)
    asking_grad, mem_grad = attend_backward(
        "all", asking, mem_near, mem_far, cross_mask, cross_wide, cross_lse, crossed_grad
    )
    mem_grad = mem_grad[::-1]
    memory_mine, memory_other, leaving = all_rows(w_e["cross"], mem_grad, None)

    def two_sided(left, left_grad, right, right_grad):
        return lambda r: jnp.concatenate([dot(left, left_grad[r], 0, 1), dot(right, right_grad[r], 0, 1)], axis=1)

    grad_cross_d = chip_total(two_sided(first_low, asking_grad, answer_grad, crossed), False)
    memory_set = jnp.concatenate([memory_near, memory_far])
    grad_cross_e = chip_total(lambda r: dot(memory_set, mem_grad[r], 0, 0), True)
    back_zero, dnorm_d0 = norm_back(
        back_one + own_sum(project(asking_grad, w_d["cross"], 0)), dec_kept_zero, norm_d[0]
    )
    mixed_grad = chip(tie(back_zero, leaving).astype(BF))
    ctx_grad = project_back(mixed_grad, w_d["qp"], heads)
    dec_dq, dec_dkv = attend_backward("causal", dec_q, dec_near, dec_far, dec_mask, dec_wide, dec_lse, ctx_grad)
    target_mine, target_other, leaving = all_rows(w_d["kv"], dec_dkv, project(dec_dq, w_d["qp"], 0))
    grad_qp_d = chip_total(two_sided(tgt_low_chip, dec_dq, mixed_grad, dec_ctx), False)
    grad_kv_d = chip_total(lambda r: dot(tgt_low, dec_dkv[r], 0, 0), True)

    memory_grad = memory_mine + tie(memory_other, dec_dq[0]).astype(F32)
    back_two, dnorm_e2 = norm_back(memory_grad * src_valid, enc_kept_two, norm_e[2])
    back, grad_up_e, grad_down_e = feed_back(
        middle_low, enc_active, enc_slope, chip(back_two.astype(BF)), w_e["up"], w_e["down"]
    )
    back_one, dnorm_e1 = norm_back(back_two + back, enc_kept_one, norm_e[1])
    mixed_grad = chip(back_one.astype(BF))
    ctx_grad = project_back(mixed_grad, w_e["qp"], heads)
    enc_dq, enc_dkv = attend_backward("window", enc_q, enc_near, enc_far, enc_mask, enc_wide, enc_lse, ctx_grad)
    target_grad = (back_zero + target_mine + tie(target_other, enc_dq[0]).astype(F32)).astype(BF)
    normed_mine, normed_other, leaving = all_rows(w_e["kv"], enc_dkv, project(enc_dq, w_e["qp"], 0))
    grad_qp_e = chip_total(two_sided(low_chip, enc_dq, mixed_grad, enc_ctx), False)
    grad_kv_e = chip_total(lambda r: dot(normed_low, enc_dkv[r], 0, 0), True)

    grad_up_d, grad_down_d = (grad_up_d(asking_grad[0]), grad_down_d(asking_grad[0]))
    grad_cross_d = grad_cross_d(dec_dq[0])
    grad_cross_e = grad_cross_e(dec_dq[0])
    grad_qp_d, grad_kv_d = (grad_qp_d(back_two), grad_kv_d(back_two))
    grad_up_e, grad_down_e = (grad_up_e(enc_dq[0]), grad_down_e(enc_dq[0]))
    grad_qp_e, grad_kv_e = (grad_qp_e(leaving), grad_kv_e(leaving))
    normed_grad = normed_mine + tie(normed_other, grad_kv_e).astype(F32)
    back_zero, dnorm_e0 = norm_back(back_one + normed_grad, enc_kept_zero, norm_e[0])
    source_grad = back_zero.astype(BF)

    dec_feed = cut_scatter([grad_up_d, grad_down_d], False)
    dec_rest = cut_scatter([grad_cross_d, grad_kv_d, grad_qp_d], False)
    dec_sum = jnp.concatenate([dec_rest, dec_feed], axis=1)
    dec_sum = dec_sum + crossing(dec_sum.astype(BF), 1).astype(F32)
    enc_feed = cut_scatter([grad_cross_e, grad_up_e, grad_down_e], False)
    enc_attn = cut_scatter([grad_kv_e, grad_qp_e], True)
    enc_feed = enc_feed + crossing(enc_feed.astype(BF), 0).astype(F32)
    enc_attn = enc_attn + crossing(enc_attn.astype(BF), 0).astype(F32)
    cross_width = sizes["cross"]
    cross = jnp.where(section == 0, enc_feed[:, :cross_width], dec_sum[:, :cross_width])
    attn = jnp.where(section == 0, enc_attn, dec_sum[:, cross_width : cross_width + attn_width])
    feed = jnp.where(section == 0, enc_feed[:, cross_width:], dec_sum[:, cross_width + attn_width :])
    norm_sum = everywhere(
        jnp.stack([jnp.stack([dnorm_e0, dnorm_e1, dnorm_e2]), jnp.stack([dnorm_d0, dnorm_d1, dnorm_d2])])
    )
    norm_share = lax.dynamic_slice(norm_sum, (section, 0, 0, lax.axis_index("dp") * cut), (1, 3, 2, cut))

    def everyone(rows):
        full = lax.all_gather(rows, ("section", "ty", "tc"), tiled=True)
        return full.reshape(2, -1, width)

    grad_attn = jnp.concatenate([attn[:, 2 * heads : 3 * heads], attn[:, : 2 * heads]], axis=1)
    return (
        everyone(output),
        everyone(source_grad),
        everyone(target_grad),
        grad_attn.reshape(1, cut, 3, heads),
        attn[:, 3 * heads :].T[None],
        cross.reshape(1, cut, 2, heads),
        feed[None, :, :units],
        feed[:, units:].T[None],
        norm_share,
    )


def solution(mesh):
    shape = mesh.devices.shape
    fine = Mesh(mesh.devices.reshape(shape[0], shape[1], 2, 2), ("section", "dp", "ty", "tc"))
    tensor = ("ty", "tc")
    return jax.shard_map(
        local,
        mesh=fine,
        in_specs=(
            P("dp", None, None),
            P("dp", None, None),
            P("dp"),
            P("dp"),
            P("dp", None),
            P("section", "dp", None, tensor),
            P("section", tensor, "dp"),
            P("section", "dp", None, tensor),
            P("section", "dp", tensor),
            P("section", tensor, "dp"),
            P("section", None, None, None),
            P("dp", None, None),
        ),
        out_specs=(
            P("dp", None, None),
            P("dp", None, None),
            P("dp", None, None),
            P("section", "dp", None, tensor),
            P("section", tensor, "dp"),
            P("section", "dp", None, tensor),
            P("section", "dp", tensor),
            P("section", tensor, "dp"),
            P("section", None, None, "dp"),
        ),
        check_vma=False,
    )
```

```python
import functools

import jax
import jax.numpy as jnp
from jax import lax
from jax.experimental import pallas as pl
from jax.experimental.pallas import tpu as pltpu
from jax.sharding import Mesh, PartitionSpec as P

HD = 64
WINDOW = 1024
EPS = 1e-05
MASKED = -1000000000.0
BF = jnp.bfloat16
F32 = jnp.float32
FORWARD_BLOCK = 256
BACKWARD_BLOCK = 512


def dot(a, b, ca, cb):
    return lax.dot_general(a, b, (((ca,), (cb,)), ((), ())), preferred_element_type=F32)


def fill_bias(mode, seg, place_ref, key_bias_ref, key_mark_ref, q_mark_ref, bias_ref):
    lanes = FORWARD_BLOCK
    pieces = bias_ref.shape[1] // lanes
    for at in range(0, bias_ref.shape[0], seg):
        keys = pl.ds(at, seg)
        key_bias = key_bias_ref[keys, :]
        for piece in range(pieces):
            queries = pl.ds(piece * lanes, lanes)
            if mode == "all":
                bias_ref[keys, queries] = jnp.broadcast_to(key_bias, (seg, lanes))
                continue
            key_place = place_ref[at // seg] + lax.broadcasted_iota(jnp.int32, (seg, lanes), 0)
            first = place_ref[4 + pl.program_id(0) * pieces + piece]
            query_place = first + lax.broadcasted_iota(jnp.int32, (seg, lanes), 1)
            if mode == "causal":
                allowed = key_place <= query_place
            else:
                marked = key_mark_ref[keys, :] + q_mark_ref[:, queries] > 0.5
                allowed = (jnp.abs(key_place - query_place) <= WINDOW // 2) | marked
            bias_ref[keys, queries] = jnp.where(allowed, key_bias, MASKED)


def attend_forward_kernel(mode, chunks, place_ref, *refs):
    q_refs = refs[:chunks]
    near_refs = refs[chunks : 2 * chunks]
    far_refs = refs[2 * chunks : 3 * chunks]
    key_bias_ref, key_mark_ref, q_mark_ref = refs[3 * chunks : 3 * chunks + 3]
    outs = refs[3 * chunks + 3 :]
    ctx_refs, wide_refs, lse_ref, bias_ref = outs[:chunks], outs[chunks : 2 * chunks], outs[2 * chunks], outs[-1]
    cut = q_refs[0].shape[0]
    half = near_refs[0].shape[1]
    step = 256
    ones = jnp.ones((16, step), BF)
    fill_bias(mode, half // 2, place_ref, key_bias_ref, key_mark_ref, q_mark_ref, bias_ref)
    for chunk in range(chunks):
        for inner in range(cut // HD):
            feats = pl.ds(inner * HD, HD)
            value_feats = pl.ds(cut + inner * HD, HD)
            query = q_refs[chunk][feats, :]
            pieces = []
            highest = None
            for kv_ref, base in ((near_refs[chunk], 0), (far_refs[chunk], half)):
                for at in range(0, half, step):
                    keys = pl.ds(at, step)
                    scores = dot(kv_ref[feats, keys], query, 0, 0) + bias_ref[pl.ds(base + at, step), :]
                    top = jnp.max(scores, axis=0, keepdims=True)
                    highest = top if highest is None else jnp.maximum(highest, top)
                    pieces.append((scores, kv_ref, keys))
            total = None
            summed = None
            for scores, kv_ref, keys in pieces:
                lifted = jnp.exp(scores - highest)
                count = jnp.sum(lifted, axis=0, keepdims=True)
                summed = count if summed is None else summed + count
                value = jnp.concatenate([kv_ref[value_feats, keys], ones], axis=0)
                part = dot(value, lifted.astype(BF), 1, 0)
                total = part if total is None else total + part
            context = total[:HD] / total[HD : HD + 1]
            ctx_refs[chunk][feats, :] = context.astype(BF)
            wide_refs[chunk][feats, :] = context
            head = chunk * (cut // HD) + inner
            lse_ref[head : head + 1, :] = highest + jnp.log(summed)


def mask_specs(half, block):
    return [
        pl.BlockSpec((2 * half, 1), lambda b, p: (0, 0)),
        pl.BlockSpec((2 * half, 1), lambda b, p: (0, 0)),
        pl.BlockSpec((1, block), lambda b, p: (0, b)),
    ]


def attend_forward(mode, q, near, far, mask):
    chunks = len(q)
    cut, rows = q[0].shape
    half = near[0].shape[1]
    heads = chunks * cut // HD
    side = pl.BlockSpec((2 * cut, half), lambda b, p: (0, 0))
    lane = pl.BlockSpec((cut, FORWARD_BLOCK), lambda b, p: (0, b))
    out = pl.pallas_call(
        functools.partial(attend_forward_kernel, mode, chunks),
        grid_spec=pltpu.PrefetchScalarGridSpec(
            num_scalar_prefetch=1,
            grid=(rows // FORWARD_BLOCK,),
            in_specs=[lane] * chunks + [side] * (2 * chunks) + mask_specs(half, FORWARD_BLOCK),
            out_specs=[lane] * (2 * chunks) + [pl.BlockSpec((heads, FORWARD_BLOCK), lambda b, p: (0, b))],
            scratch_shapes=[pltpu.VMEM((2 * half, FORWARD_BLOCK), F32)],
        ),
        out_shape=[jax.ShapeDtypeStruct((cut, rows), BF)] * chunks
        + [jax.ShapeDtypeStruct((cut, rows), F32)] * chunks
        + [jax.ShapeDtypeStruct((heads, rows), F32)],
        compiler_params=pltpu.CompilerParams(vmem_limit_bytes=48 * 1024 * 1024),
        cost_estimate=pl.CostEstimate(
            flops=cut * rows, bytes_accessed=cut * rows, transcendentals=0
        ),
    )(mask[0], *q, *near, *far, *mask[1:])
    return (out[:chunks], out[chunks : 2 * chunks], out[2 * chunks])


def attend_backward_kernel(mode, chunks, place_ref, *refs):
    q_refs = refs[:chunks]
    near_refs = refs[chunks : 2 * chunks]
    far_refs = refs[2 * chunks : 3 * chunks]
    key_bias_ref, key_mark_ref, q_mark_ref = refs[3 * chunks : 3 * chunks + 3]
    rest = refs[3 * chunks + 3 :]
    wide_refs, lse_ref, do_refs = rest[:chunks], rest[chunks], rest[chunks + 1 : 2 * chunks + 1]
    outs = rest[2 * chunks + 1 :]
    dq_refs, dkv_refs, sums, bias_ref = outs[:chunks], outs[chunks : 2 * chunks], outs[2 * chunks : 3 * chunks], outs[-1]
    cut = q_refs[0].shape[0]
    heads = cut // HD
    half = near_refs[0].shape[1]
    block = pl.program_id(0)
    fill_bias(mode, half // 2, place_ref, key_bias_ref, key_mark_ref, q_mark_ref, bias_ref)

    @pl.when(block == 0)
    def _():
        for total in sums:
            total[...] = jnp.zeros_like(total)

    def placed(feats, slot):
        blank = jnp.zeros_like(feats)
        pair = [feats, blank] if slot % 2 == 0 else [blank, feats]
        return jnp.concatenate(pair, axis=0).T

    for chunk in range(chunks):
        for inner in range(heads):
            feats = pl.ds(inner * HD, HD)
            value_feats = pl.ds(cut + inner * HD, HD)
            query = q_refs[chunk][feats, :]
            grad = do_refs[chunk][feats, :]
            q_side = placed(query, inner)
            do_side = placed(grad, heads + inner)
            key_lanes = pl.ds(inner // 2 * 2 * HD, 2 * HD)
            value_lanes = pl.ds((heads + inner) // 2 * 2 * HD, 2 * HD)
            head = chunk * heads + inner
            lse = lse_ref[head : head + 1, :]
            delta = jnp.sum(grad.astype(F32) * wide_refs[chunk][feats, :], axis=0, keepdims=True)
            total = None
            for kv_ref, base in ((near_refs[chunk], 0), (far_refs[chunk], half)):
                keys = pl.ds(base, half)
                scores = dot(kv_ref[feats, :], query, 0, 0) + bias_ref[keys, :]
                probs = jnp.exp(scores - lse)
                grad_probs = dot(kv_ref[value_feats, :], grad, 0, 0)
                grad_scores = (probs * (grad_probs - delta)).astype(BF)
                sums[chunk][keys, value_lanes] += dot(probs.astype(BF), do_side, 1, 0)
                sums[chunk][keys, key_lanes] += dot(grad_scores, q_side, 1, 0)
                part = dot(kv_ref[feats, :], grad_scores, 1, 0)
                total = part if total is None else total + part
            dq_refs[chunk][feats, :] = (total * (HD**-0.5)).astype(BF)

    @pl.when(block == pl.num_programs(0) - 1)
    def _():
        for chunk in range(chunks):
            dkv_refs[chunk][...] = sums[chunk][...].astype(BF)


def attend_backward(mode, q, near, far, mask, wide, lse, grad):
    chunks = len(q)
    cut, rows = q[0].shape
    half = near[0].shape[1]
    heads = chunks * cut // HD
    side = pl.BlockSpec((2 * cut, half), lambda b, p: (0, 0))
    lane = pl.BlockSpec((cut, BACKWARD_BLOCK), lambda b, p: (0, b))
    key_side = pl.BlockSpec((2 * half, 2 * cut), lambda b, p: (0, 0))
    out = pl.pallas_call(
        functools.partial(attend_backward_kernel, mode, chunks),
        grid_spec=pltpu.PrefetchScalarGridSpec(
            num_scalar_prefetch=1,
            grid=(rows // BACKWARD_BLOCK,),
            in_specs=[lane] * chunks
            + [side] * (2 * chunks)
            + mask_specs(half, BACKWARD_BLOCK)
            + [lane] * chunks
            + [pl.BlockSpec((heads, BACKWARD_BLOCK), lambda b, p: (0, b))]
            + [lane] * chunks,
            out_specs=[lane] * chunks + [key_side] * chunks,
            scratch_shapes=[pltpu.VMEM((2 * half, 2 * cut), F32)] * chunks + [pltpu.VMEM((2 * half, BACKWARD_BLOCK), F32)],
        ),
        out_shape=[jax.ShapeDtypeStruct((cut, rows), BF)] * chunks
        + [jax.ShapeDtypeStruct((2 * half, 2 * cut), BF)] * chunks,
        compiler_params=pltpu.CompilerParams(vmem_limit_bytes=56 * 1024 * 1024),
        cost_estimate=pl.CostEstimate(
            flops=cut * rows, bytes_accessed=cut * rows, transcendentals=0
        ),
    )(mask[0], *q, *near, *far, *mask[1:], *wide, lse, *grad)
    return (out[:chunks], out[chunks:])


def assemble_kernel(widths, at_ref, *refs):
    step = pl.program_id(0)
    slots, outs = refs[:4], refs[4:]
    for index in range(4):

        @pl.when(step == index)
        def _():
            start = 0
            for width, out in zip(widths, outs):
                out[...] = slots[index][:, start : start + width]
                start += width


def assemble(at, slots, widths):
    rows, columns = slots[0].shape
    return pl.pallas_call(
        functools.partial(assemble_kernel, widths),
        grid_spec=pltpu.PrefetchScalarGridSpec(
            num_scalar_prefetch=1,
            grid=(4,),
            in_specs=[pl.BlockSpec((rows, columns), lambda k, at: (0, 0))] * 4,
            out_specs=[pl.BlockSpec((rows, width), lambda k, at: ((at[0] + k) % 4, 0)) for width in widths],
        ),
        out_shape=[jax.ShapeDtypeStruct((4 * rows, width), BF) for width in widths],
        compiler_params=pltpu.CompilerParams(vmem_limit_bytes=40 * 1024 * 1024),
    )(at.reshape(1), *slots)


def layer_norm(z, norm):
    center = z - jnp.mean(z, axis=-1, keepdims=True)
    inverse = lax.rsqrt(jnp.mean(center * center, axis=-1, keepdims=True) + EPS)
    scaled = center * inverse
    return (scaled * norm[0] + norm[1], (scaled, inverse))


def norm_back(grad, kept, norm):
    scaled, inverse = kept
    inner = grad * norm[0]
    back = inverse * (
        inner
        - jnp.mean(inner, axis=-1, keepdims=True)
        - scaled * jnp.mean(inner * scaled, axis=-1, keepdims=True)
    )
    return (back, jnp.stack([jnp.sum(grad * scaled, axis=0), jnp.sum(grad, axis=0)]))


def gelu_both(raised):
    rise = 0.5 * (1.0 + lax.erf(raised * (0.5**0.5)))
    slope = rise + raised * jnp.exp(-0.5 * raised * raised) * 0.3989422804014327
    return ((raised * rise).astype(BF), slope.astype(BF))


def hop(value, axis, pairs):
    return lax.ppermute(value, axis, pairs)


def swap(value, axis):
    return hop(value, axis, [(0, 1), (1, 0)])


def crossing(value, to):
    pairs = [(2 * (1 - to) + y, 2 * to + 1 - y) for y in range(2)]
    return hop(value, ("section", "ty"), pairs)


def cut_gather(shard, widths, quick):
    if lax.axis_size("dp") != 4 or not quick:
        full = lax.all_gather(shard, "dp", tiled=True)
        edges = [sum(widths[:i]) for i in range(1, len(widths))]
        return jnp.split(full, edges, axis=1)
    at = lax.axis_index("dp")
    up = hop(shard, "dp", [(j, (j - 1) % 4) for j in range(4)])
    down = hop(shard, "dp", [(j, (j + 1) % 4) for j in range(4)])
    from_up = hop(up, "dp", [(1, 0), (2, 1)])
    from_down = hop(down, "dp", [(1, 2), (2, 3)])
    far = jnp.where(at < 2, from_up, from_down)
    return assemble(at, (shard, up, far, down), widths)


def cut_scatter(tensors, quick):
    size = lax.axis_size("dp")
    if size != 4 or not quick:
        full = jnp.concatenate(tensors, axis=1)
        return lax.psum_scatter(full, "dp", tiled=True).astype(F32)
    at = lax.axis_index("dp")
    rows = tensors[0].shape[0] // 4

    def slot(k):
        start = lax.rem(at + k, 4) * rows
        return jnp.concatenate([lax.dynamic_slice_in_dim(t, start, rows, 0) for t in tensors], axis=1)

    far = slot(2)
    to_up = hop(far, "dp", [(0, 1), (1, 2)])
    to_down = hop(far, "dp", [(2, 1), (3, 2)])
    ahead = add_low(slot(1), to_up)
    behind = add_low(slot(3), to_down)
    from_behind = hop(ahead, "dp", [(j, (j + 1) % 4) for j in range(4)])
    from_ahead = hop(behind, "dp", [(j, (j - 1) % 4) for j in range(4)])
    return slot(0).astype(F32) + from_behind.astype(F32) + from_ahead.astype(F32)


def add_low(a, b):
    return (a.astype(F32) + b.astype(F32)).astype(BF)


def everywhere(value):
    for axis in ("tc", "ty", "section"):
        value = value + swap(value, axis)
    size = lax.axis_size("dp")
    reach = 1
    while reach < size:
        value = value + hop(value, "dp", [(j, j ^ reach) for j in range(size)])
        reach *= 2
    return value


def tie(value, token):
    first = token[(0,) * token.ndim]
    return jnp.where(first == first, value, jnp.zeros_like(value))


def total_of(parts):
    total = parts[0]
    for part in parts[1:]:
        total = total + part
    return total


def local(source, target, src_len, tgt_len, global_mask, attn_w, proj_w, cross_w, up_w, down_w, norms, dec_cot):
    section = lax.axis_index("section")
    y = lax.axis_index("ty")
    c = lax.axis_index("tc")
    src_rows = source.shape[1]
    tgt_rows = target.shape[1]
    width = source.shape[2]
    src_own = src_rows // 4
    tgt_own = tgt_rows // 4
    cut = attn_w.shape[1]
    heads = attn_w.shape[3]
    units = up_w.shape[2]
    scale = HD**-0.5

    def pick(array):
        return lax.dynamic_index_in_dim(array, section, 0, keepdims=False)

    src_length = pick(src_len)
    tgt_length = pick(tgt_len)
    order = jnp.stack([2 * y + c, 2 * y + 1 - c, 2 * (1 - y) + c, 2 * (1 - y) + 1 - c]).astype(jnp.int32)

    def ordered(array):
        size = array.shape[0] // 4
        return jnp.concatenate([lax.dynamic_slice_in_dim(array, order[i] * size, size, 0) for i in range(4)])

    src_place = ordered(jnp.arange(src_rows, dtype=jnp.int32))
    tgt_place = ordered(jnp.arange(tgt_rows, dtype=jnp.int32))
    src_valid = (src_place[:src_own] < src_length).astype(F32)[:, None]
    tgt_valid = (tgt_place[:tgt_own] < tgt_length).astype(F32)[:, None]
    marks = ordered(pick(global_mask) > 0).astype(F32)
    src_bias = jnp.where(src_place < src_length, 0.0, MASKED).astype(F32)[:, None]
    tgt_bias = jnp.where(tgt_place < tgt_length, 0.0, MASKED).astype(F32)[:, None]

    def places(place, queries):
        return jnp.concatenate([place[:: place.shape[0] // 4], queries[::FORWARD_BLOCK]])

    src_chip = 2 * src_own
    tgt_chip = 2 * tgt_own
    enc_mask = (places(src_place, src_place[:src_chip]), src_bias, marks[:, None], marks[None, :src_chip])
    dec_mask = (places(tgt_place, tgt_place[:tgt_chip]), tgt_bias, tgt_bias, tgt_bias[:tgt_chip].T)
    cross_mask = (places(src_place, tgt_place[:tgt_chip]), src_bias, src_bias, dec_mask[3])

    flat = attn_w.reshape(cut, 3 * heads)
    kv_cut = flat[:, heads:]
    qp_cut = jnp.concatenate([flat[:, :heads], proj_w[0].T], axis=1)
    up_cut = up_w.reshape(cut, units)
    down_cut = down_w[0].T
    cross_cut = cross_w.reshape(cut, 2 * heads)

    cuts = {"kv": kv_cut, "qp": qp_cut, "up": up_cut, "down": down_cut, "cross": cross_cut}
    sizes = {name: value.shape[1] for name, value in cuts.items()}

    def packed(names):
        return jnp.concatenate([cuts[name] for name in names], axis=1)

    def spread(layer, names, full):
        chunks = {}
        for name, mine in zip(names, full):
            by_x = name in ("kv", "up") or (name == "cross" and layer == 0)
            chunks[name] = [mine, swap(mine, "section" if by_x else "ty")]
        return chunks

    norms_all = jnp.stack([norms[0], swap(norms[0], "section")])
    norms_all = jnp.where(section == 0, norms_all, norms_all[::-1])
    norm_e = norms_all[0]
    norm_d = norms_all[1]

    attn_names, feed_names = ("kv", "qp"), ("up", "down")
    attn_width = sizes["kv"] + sizes["qp"]
    feed_width = sizes["up"] + sizes["down"]
    everything = packed(attn_names + feed_names + ("cross",))
    came = hop(everything, ("section", "ty"), [(2 * x + v, 2 * (1 - x) + 1 - v) for x in range(2) for v in range(2)])
    all_e = jnp.where(section == 0, everything, came)
    all_d = jnp.where(section == 1, everything, came)

    full = cut_gather(all_e[:, :attn_width], [sizes[name] for name in attn_names], True)
    w_e = spread(0, attn_names, full)
    shard = all_e[:, attn_width : attn_width + feed_width]
    w_e.update(spread(0, feed_names, cut_gather(shard, [sizes[name] for name in feed_names], False)))
    token = w_e["up"][0]
    shard = jnp.concatenate([all_e[:, attn_width + feed_width :], all_d[:, :attn_width]], axis=1)
    full = cut_gather(tie(shard, token), [sizes["cross"], sizes["kv"], sizes["qp"]], False)
    w_e.update(spread(0, ("cross",), full[:1]))
    w_d = spread(1, attn_names, full[1:])
    token = w_d["kv"][0]
    names = ("cross",) + feed_names
    shard = jnp.concatenate([all_d[:, attn_width + feed_width :], all_d[:, attn_width : attn_width + feed_width]], axis=1)
    w_d.update(spread(1, names, cut_gather(tie(shard, token), [sizes[name] for name in names], False)))

    both = range(2)

    def key_values(weights, rows):
        return [dot(weights[r], rows, 0, 1).astype(BF) for r in both]

    def queries(weights, rows):
        return [(dot(weights[r][:, :heads], rows, 0, 1) * scale).astype(BF) for r in both]

    def chip(rows):
        return jnp.concatenate([rows, swap(rows, "tc")])

    def own_sum(partial_rows):
        mine = partial_rows.shape[0] // 2
        return partial_rows[:mine] + swap(partial_rows[mine:].astype(BF), "tc").astype(F32)

    def feed_forward(low, up, down):
        active, slope, parts = [], [], []
        for r in both:
            act, rise = gelu_both(dot(low, up[r], 1, 0))
            active.append(act)
            slope.append(rise)
            parts.append(dot(act, down[r], 1, 1))
        return (active, slope, own_sum(total_of(parts)))

    def chip_total(partial_of, by_x):
        other = swap(partial_of(1).astype(BF), "section" if by_x else "ty")

        def finish(token):
            return (partial_of(0) + tie(other, token).astype(F32)).astype(BF)

        return finish

    def feed_back(low, active, slope, lowered_grad, up, down):
        raised = []
        for r in both:
            grad_active = dot(lowered_grad, down[r], 1, 0)
            raised.append((grad_active * slope[r].astype(F32)).astype(BF))
        back = own_sum(total_of([dot(raised[r], up[r], 1, 1) for r in both]))
        grad_up = chip_total(lambda r: dot(low, raised[r], 0, 0), True)
        grad_down = chip_total(lambda r: dot(lowered_grad, active[r], 0, 0), False)
        return (back, grad_up, grad_down)

    def project(ctx, weights, start):
        return total_of([dot(ctx[r], weights[r][:, start : start + heads], 0, 1) for r in both])

    def project_back(rows, weights, start):
        return [dot(weights[r][:, start : start + heads], rows, 0, 1).astype(BF) for r in both]

    def all_rows(weights, grads, more):
        partial_rows = total_of([dot(grads[r], weights[r], 1, 1) for r in both])
        size = partial_rows.shape[0] // 4
        parts = [partial_rows[i * size : (i + 1) * size] for i in range(4)]
        if more is not None:
            parts = [parts[0] + more[:size], parts[1] + more[size:], parts[2], parts[3]]
        from_core = swap(jnp.concatenate([parts[1], parts[3]]).astype(BF), "tc").astype(F32)
        leaving = (parts[2] + from_core[size:]).astype(BF)
        return (parts[0] + from_core[:size], swap(leaving, "ty"), leaving)

    normed, kept = layer_norm(ordered(pick(source)).astype(F32), norm_e[0])
    enc_kept_zero = (kept[0][:src_own], kept[1][:src_own])
    normed_low = normed.astype(BF)
    normed_mine = normed[:src_own]
    low_chip = normed_low[:src_chip]
    enc_near = key_values(w_e["kv"], low_chip)
    enc_far = key_values(w_e["kv"], normed_low[src_chip:])
    enc_q = queries(w_e["qp"], low_chip)
    enc_ctx, enc_wide, enc_lse = attend_forward("window", enc_q, enc_near, enc_far, enc_mask)
    middle, enc_kept_one = layer_norm(normed_mine + own_sum(project(enc_ctx, w_e["qp"], heads)), norm_e[1])
    middle_low = chip(middle.astype(BF))
    enc_active, enc_slope, lowered = feed_forward(middle_low, w_e["up"], w_e["down"])
    memory, enc_kept_two = layer_norm(middle + lowered, norm_e[2])
    memory_low = (memory * src_valid).astype(BF)
    memory_near = chip(memory_low)
    memory_far = chip(swap(memory_low, "ty"))
    mem_near = key_values(w_e["cross"], memory_near)
    mem_far = key_values(w_e["cross"], memory_far)

    tgt_low = ordered(pick(target))
    tgt_low_chip = tgt_low[:tgt_chip]
    dec_near = key_values(w_d["kv"], tgt_low_chip)
    dec_far = key_values(w_d["kv"], tgt_low[tgt_chip:])
    dec_q = queries(w_d["qp"], tgt_low_chip)
    dec_ctx, dec_wide, dec_lse = attend_forward("causal", dec_q, dec_near, dec_far, dec_mask)
    first, dec_kept_zero = layer_norm(
        tgt_low[:tgt_own].astype(F32) + own_sum(project(dec_ctx, w_d["qp"], heads)), norm_d[0]
    )
    first_low = chip(first.astype(BF))
    asking = queries(w_d["cross"], first_low)
    mem_near, mem_far = (mem_near[::-1], mem_far[::-1])
    crossed, cross_wide, cross_lse = attend_forward("all", asking, mem_near, mem_far, cross_mask)
    second, dec_kept_one = layer_norm(first + own_sum(project(crossed, w_d["cross"], heads)), norm_d[1])
    second_low = chip(second.astype(BF))
    dec_active, dec_slope, lowered = feed_forward(second_low, w_d["up"], w_d["down"])
    result, dec_kept_two = layer_norm(second + lowered, norm_d[2])
    output = (result * tgt_valid).astype(BF)

    cotangent = lax.dynamic_slice_in_dim(pick(dec_cot), order[0] * tgt_own, tgt_own, 0).astype(F32) * tgt_valid
    back_two, dnorm_d2 = norm_back(cotangent, dec_kept_two, norm_d[2])
    back, grad_up_d, grad_down_d = feed_back(
        second_low, dec_active, dec_slope, chip(back_two.astype(BF)), w_d["up"], w_d["down"]
    )
    back_one, dnorm_d1 = norm_back(back_two + back, dec_kept_one, norm_d[1])
    answer_grad = chip(back_one.astype(BF))
    crossed_grad = project_back(answer_grad, w_d["cross"], heads)
    asking_grad, mem_grad = attend_backward(
        "all", asking, mem_near, mem_far, cross_mask, cross_wide, cross_lse, crossed_grad
    )
    mem_grad = mem_grad[::-1]
    memory_mine, memory_other, leaving = all_rows(w_e["cross"], mem_grad, None)

    def two_sided(left, left_grad, right, right_grad):
        return lambda r: jnp.concatenate([dot(left, left_grad[r], 0, 1), dot(right, right_grad[r], 0, 1)], axis=1)

    grad_cross_d = chip_total(two_sided(first_low, asking_grad, answer_grad, crossed), False)
    memory_set = jnp.concatenate([memory_near, memory_far])
    grad_cross_e = chip_total(lambda r: dot(memory_set, mem_grad[r], 0, 0), True)
    back_zero, dnorm_d0 = norm_back(
        back_one + own_sum(project(asking_grad, w_d["cross"], 0)), dec_kept_zero, norm_d[0]
    )
    mixed_grad = chip(tie(back_zero, leaving).astype(BF))
    ctx_grad = project_back(mixed_grad, w_d["qp"], heads)
    dec_dq, dec_dkv = attend_backward("causal", dec_q, dec_near, dec_far, dec_mask, dec_wide, dec_lse, ctx_grad)
    target_mine, target_other, leaving = all_rows(w_d["kv"], dec_dkv, project(dec_dq, w_d["qp"], 0))
    grad_qp_d = chip_total(two_sided(tgt_low_chip, dec_dq, mixed_grad, dec_ctx), False)
    grad_kv_d = chip_total(lambda r: dot(tgt_low, dec_dkv[r], 0, 0), True)

    memory_grad = memory_mine + tie(memory_other, dec_dq[0]).astype(F32)
    back_two, dnorm_e2 = norm_back(memory_grad * src_valid, enc_kept_two, norm_e[2])
    back, grad_up_e, grad_down_e = feed_back(
        middle_low, enc_active, enc_slope, chip(back_two.astype(BF)), w_e["up"], w_e["down"]
    )
    back_one, dnorm_e1 = norm_back(back_two + back, enc_kept_one, norm_e[1])
    mixed_grad = chip(back_one.astype(BF))
    ctx_grad = project_back(mixed_grad, w_e["qp"], heads)
    target_grad = (back_zero + target_mine + tie(target_other, back_one).astype(F32)).astype(BF)
    ctx_grad[0] = tie(ctx_grad[0], target_grad)
    enc_dq, enc_dkv = attend_backward("window", enc_q, enc_near, enc_far, enc_mask, enc_wide, enc_lse, ctx_grad)
    normed_mine, normed_other, leaving = all_rows(w_e["kv"], enc_dkv, project(enc_dq, w_e["qp"], 0))
    grad_qp_e = chip_total(two_sided(low_chip, enc_dq, mixed_grad, enc_ctx), True)
    grad_kv_e = chip_total(lambda r: dot(normed_low, enc_dkv[r], 0, 0), True)

    grad_up_d, grad_down_d = (grad_up_d(asking_grad[0]), grad_down_d(asking_grad[0]))
    grad_cross_d = grad_cross_d(dec_dq[0])
    grad_cross_e = grad_cross_e(dec_dq[0])
    grad_qp_d, grad_kv_d = (grad_qp_d(back_two), grad_kv_d(back_two))
    grad_up_e, grad_down_e = (grad_up_e(enc_dq[0]), grad_down_e(enc_dq[0]))
    grad_qp_e, grad_kv_e = (grad_qp_e(leaving), grad_kv_e(leaving))
    normed_grad = normed_mine + tie(normed_other, grad_kv_e).astype(F32)
    back_zero, dnorm_e0 = norm_back(back_one + normed_grad, enc_kept_zero, norm_e[0])
    source_grad = back_zero.astype(BF)

    dec_feed = cut_scatter([grad_up_d, grad_down_d], False)
    dec_rest = cut_scatter([grad_cross_d, grad_kv_d, grad_qp_d], False)
    feed_more = crossing(dec_feed.astype(BF), 1)
    rest_more = crossing(dec_rest.astype(BF), 1)
    dec_feed = dec_feed + feed_more.astype(F32)
    dec_rest = dec_rest + rest_more.astype(F32)
    enc_feed = cut_scatter([grad_cross_e, grad_up_e, grad_down_e], False)
    enc_attn = cut_scatter([grad_kv_e, grad_qp_e], True)
    enc_feed = enc_feed + crossing(enc_feed.astype(BF), 0).astype(F32)
    norm_sum = everywhere(
        jnp.stack([jnp.stack([dnorm_e0, dnorm_e1, dnorm_e2]), jnp.stack([dnorm_d0, dnorm_d1, dnorm_d2])])
    )
    norm_share = lax.dynamic_slice(norm_sum, (section, 0, 0, lax.axis_index("dp") * cut), (1, 3, 2, cut))
    enc_attn = enc_attn + crossing(tie(enc_attn, norm_sum).astype(BF), 0).astype(F32)
    cross_width = sizes["cross"]
    cross = jnp.where(section == 0, enc_feed[:, :cross_width], dec_rest[:, :cross_width])
    attn = jnp.where(section == 0, enc_attn, dec_rest[:, cross_width:])
    feed = jnp.where(section == 0, enc_feed[:, cross_width:], dec_feed)
    def everyone(rows):
        full = lax.all_gather(rows, ("section", "ty", "tc"), tiled=True)
        return full.reshape(2, -1, width)

    grad_attn = jnp.concatenate([attn[:, 2 * heads : 3 * heads], attn[:, : 2 * heads]], axis=1)
    return (
        everyone(output),
        everyone(source_grad),
        everyone(target_grad),
        grad_attn.reshape(1, cut, 3, heads),
        attn[:, 3 * heads :].T[None],
        cross.reshape(1, cut, 2, heads),
        feed[None, :, :units],
        feed[:, units:].T[None],
        norm_share,
    )


def solution(mesh):
    shape = mesh.devices.shape
    fine = Mesh(mesh.devices.reshape(shape[0], shape[1], 2, 2), ("section", "dp", "ty", "tc"))
    tensor = ("ty", "tc")
    return jax.shard_map(
        local,
        mesh=fine,
        in_specs=(
            P("dp", None, None),
            P("dp", None, None),
            P("dp"),
            P("dp"),
            P("dp", None),
            P("section", "dp", None, tensor),
            P("section", tensor, "dp"),
            P("section", "dp", None, tensor),
            P("section", "dp", tensor),
            P("section", tensor, "dp"),
            P("section", None, None, None),
            P("dp", None, None),
        ),
        out_specs=(
            P("dp", None, None),
            P("dp", None, None),
            P("dp", None, None),
            P("section", "dp", None, tensor),
            P("section", tensor, "dp"),
            P("section", "dp", None, tensor),
            P("section", "dp", tensor),
            P("section", tensor, "dp"),
            P("section", None, None, "dp"),
        ),
        check_vma=False,
    )
```
